512 devices in a mesh: node: 64 (over z, y_hi, x), local: 8 (over y_lo, core).
Axes of the slice: x: 4, y: 8 (y_hi: 2, y_lo: 4; y = y_hi * 4 + y_lo), z: 8, core: 2. Of those that a mesh axis runs over, the one named last changes fastest.
Arguments:
- normed_input: bfloat16 [131072, 4096], P(('node', 'local')), may hold values from -60 to 60
- key_weight: bfloat16 [4096, 512], P(('node', 'local')), may hold values from -0.09375 to 0.09375
- key_cotangent: bfloat16 [131072, 512], P(('node', 'local')), may hold values from -60 to 60
Outputs:
- keys: bfloat16 [131072, 512], P(('node', 'local'))
- input_grad: bfloat16 [131072, 4096], P(('node', 'local'))
- weight_update: float32 [4096, 512], P(('node', 'local'))
The draws below stay inside these ranges and needn't reach their ends.
All inputs are finite; a program needn't handle non-finite values.
Results may differ from the reference program's by a relative error of at most 0.0029.
Values may be sent and summed in bfloat16 or wider, within the bound.
A program may use at most 64 MiB of HBM per device.

```python
import jax
import jax.numpy as jnp
from jax import lax

WIDTH = 4096
TOK_DEV = 256
KV_WIDTH = 512
TOKENS = 131072
N_NODE = 64
N_LOCAL = 8


def column_scales(key, count, trend, spread):
    ranks = jnp.arange(count, dtype=jnp.float32) / (count - 1)
    wobble = jax.random.uniform(key, (count,), jnp.float32)
    return jnp.exp((ranks - 0.5) * jnp.log(trend) + (wobble - 0.5) * jnp.log(spread))


def draw_normed_input(key, part):
    key = jax.random.fold_in(key, 11)
    first, second = jax.random.split(key, 2)
    base = jnp.clip(jax.random.normal(first, (TOKENS, WIDTH), jnp.float32), -4.0, 4.0)
    scales = column_scales(second, WIDTH, 3.0, 10.0)
    return (base * scales).astype(jnp.bfloat16)


def draw_key_cotangent(key, part):
    key = jax.random.fold_in(key, 12)
    first, second = jax.random.split(key, 2)
    base = jnp.clip(jax.random.normal(first, (TOKENS, KV_WIDTH), jnp.float32), -4.0, 4.0)
    scales = column_scales(second, KV_WIDTH, 3.0, 10.0)
    return (base * scales).astype(jnp.bfloat16)


def levels(stream_key, shape, cuts, smallest, high):
    def one(dim, parts):
        heights = jax.random.uniform(jax.random.fold_in(jax.random.fold_in(stream_key, 6), dim), (parts,), jnp.float32, smallest / len(cuts), high / len(cuts))
        return jnp.repeat(jnp.exp(heights), shape[dim] // parts).reshape((-1,) + (1,) * (len(shape) - dim - 1))

    factor_of = one(*cuts[0])
    for cut in cuts[1:]:
        factor_of = factor_of * one(*cut)
    return factor_of


def gaussian(rng, dims, scale, reach, shards=(), held_as=jnp.bfloat16):
    factor_of = levels(rng, dims, shards, -0.22, 0.18) if shards else 1.0
    entries = jax.random.normal(rng, dims, jnp.float32) * scale * factor_of
    return jnp.minimum(jnp.maximum(entries, -reach), reach).astype(held_as)


def setup_inputs(seed: int = 0) -> dict:
    key_of = jax.random.split(jax.random.key(seed), 4)
    normed_input = draw_normed_input(jax.random.fold_in(key_of[3], 71), 0)
    key_weight = gaussian(key_of[1], (WIDTH, KV_WIDTH), WIDTH ** -0.5, 0.09375, ((0, 512),))
    key_cotangent = draw_key_cotangent(jax.random.fold_in(key_of[3], 71), 0)
    return {"normed_input": normed_input, "key_weight": key_weight, "key_cotangent": key_cotangent}


def reference(normed_input, key_weight, key_cotangent):
    keys = jnp.dot(normed_input, key_weight, preferred_element_type=jnp.float32).astype(jnp.bfloat16)
    input_grad = jnp.dot(key_cotangent, key_weight.T, preferred_element_type=jnp.float32).astype(jnp.bfloat16)
    blocks = N_NODE * N_LOCAL
    input_blocks = normed_input.reshape(blocks, TOK_DEV, WIDTH)
    cotangent_blocks = key_cotangent.reshape(blocks, TOK_DEV, KV_WIDTH)

    def accumulate(total, pair):
        inputs, cotangent = pair
        term = jnp.dot(inputs.T, cotangent, preferred_element_type=jnp.float32).astype(jnp.bfloat16)
        return (total + term.astype(jnp.float32), None)
    weight_grad, _ = lax.scan(accumulate, jnp.zeros((WIDTH, KV_WIDTH), jnp.float32), (input_blocks, cotangent_blocks))
    mean_square = jnp.sum(weight_grad * weight_grad) / (WIDTH * KV_WIDTH)
    weight_update = weight_grad * lax.rsqrt(mean_square + 1e-06)
    return (keys, input_grad, weight_update)
```

```python
import jax
import jax.numpy as jnp
from jax import lax
from jax.experimental import pallas as pl
from jax.experimental.pallas import tpu as pltpu
from jax.sharding import PartitionSpec as P

MESH = pl.DeviceIdType.MESH
NX, NY, NZ = 4, 8, 8
F32, BF16 = jnp.float32, jnp.bfloat16
ORDER = (4, 3, 5, 2, 6, 1, 7, 0)


def mod(a, n):
    return lax.rem(a + n, n)


def dev(x, y, z, c):
    return ((z * 2 + lax.div(y, 4)) * 4 + x, lax.rem(y, 4) * 2 + c)


def copy_to(src, dst, send_sem, recv_sem, device):
    return pltpu.make_async_remote_copy(
        src_ref=src,
        dst_ref=dst,
        send_sem=send_sem,
        recv_sem=recv_sem,
        device_id=device,
        device_id_type=MESH,
    )


def kernel(
    x_ref, w_ref, c_ref, keys_ref, grad_ref, update_ref,
    weight, shard, shard_in, away, pair_in, term, ring_in, block, block_in,
    slab, slab_in, mine, mine_in, squares, squares_in, keys_sum,
    shard_s, shard_r, pair_s, pair_r, gz_s, gz_r, gy_s, gy_r, gx_s, gx_r, gf_s, gf_r, gc_s, gc_r,
    ring_s, ring_r, block_s, block_r, slab_s, slab_r, mine_s, mine_r, sq_s, sq_r,
):
    node, local = lax.axis_index("node"), lax.axis_index("local")
    x = lax.rem(node, 4)
    y = lax.rem(lax.div(node, 4), 2) * 4 + lax.div(local, 2)
    z = lax.div(node, 8)
    c = lax.rem(local, 2)
    sib = 1 - c
    sibling = dev(x, y, z, sib)
    along_x = lambda k: dev(mod(x + k, NX), y, z, c)
    along_y = lambda k: dev(x, mod(y + k, NY), z, c)
    along_z = lambda k: dev(x, y, mod(z + k, NZ), c)
    place = (z, y)
    along = (along_z, along_y)
    across = (along_y, along_z)
    across_place = (y, z)
    sent = []

    def start(copy):
        copy.start()
        sent.append(copy)

    barrier = pltpu.get_barrier_semaphore()
    greeted = [along_z(k) for k in range(1, NZ)] + [along_y(k) for k in range(1, NY)]
    greeted += [dev(mod(x + k, NX), y, z, c) for k in range(1, NX)]
    greeted += [dev(mod(x + k, NX), y, z, sib) for k in range(NX)]
    for device in greeted:
        pl.semaphore_signal(barrier, inc=1, device_id=device, device_id_type=MESH)

    def terms_of(half, ref):
        cot = c_ref[:, pl.ds(pl.multiple_of(half * 256, 256), 256)]

        def one(zb, carry):
            rows = x_ref[:, pl.ds(pl.multiple_of(zb * 512, 512), 512)]
            t = lax.dot_general(
                rows, cot, (((0,), (0,)), ((), ())), preferred_element_type=F32
            ).astype(BF16)
            ref[0, zb] = t[:, :128].reshape(2, 4, 64, 128)
            tb = t[:, 128:].reshape(2, 4, 4, 16, 128)
            for yh in range(2):
                for yl in range(4):
                    ref[1, yh * 4 + yl, lax.div(zb, 4), lax.rem(zb, 4)] = tb[yh, :, yl].reshape(64, 128)
            return carry

        lax.fori_loop(0, 8, one, 0)

    w = w_ref[...].astype(F32)
    shard[0] = w[:, :256]
    shard[1] = w[:, 256:]
    terms_of(sib, away)
    pl.semaphore_wait(barrier, len(greeted))

    start(copy_to(shard.at[sib], shard_in, shard_s, shard_r, sibling))
    pairs = {}
    for o in ORDER:
        for q in range(2):
            b = mod(place[q] + o, 8)
            pairs[q, o] = copy_to(away.at[q, b], pair_in.at[q, b], pair_s.at[q, o], pair_r.at[q, o], sibling)
            start(pairs[q, o])
    terms_of(c, term)

    yh, yl = lax.div(y, 4), lax.rem(y, 4)
    copy_to(shard.at[sib], shard_in, shard_s, shard_r, sibling).wait_recv()
    own, other = shard[c], shard_in[...]
    first = jnp.where(c == 0, own, other)
    second = jnp.where(c == 0, other, own)
    weight[c, z, yh, x, yl] = jnp.concatenate([first, second], axis=0).astype(BF16)
    for k in range(1, NZ):
        spot = weight.at[c, z, yh, x, yl]
        start(copy_to(spot, spot, gz_s.at[k - 1], gz_r.at[k - 1], along_z(k)))

    def length(sign, u):
        return 4 if (sign == 0) == (u == 0) else 3

    waited = set()

    def paired(q, o, u):
        if (q, o % 8) not in waited:
            waited.add((q, o % 8))
            pairs[q, o % 8].wait_recv()
        b = mod(place[q] + o, 8)
        return b, term[q, b, u].astype(F32) + pair_in[q, b, u].astype(F32)

    def ring_copy(q, sign, u, s, b):
        return copy_to(
            term.at[q, b, u],
            ring_in.at[q, sign, u, s - 1],
            ring_s.at[q, sign, u, s - 1],
            ring_r.at[q, sign, u, s - 1],
            along[q](1 - 2 * sign),
        )

    def ring_step(s):
        for u in range(2):
            for q in range(2):
                for sign in range(2):
                    n = length(sign, u)
                    if s > n:
                        continue
                    o = (1 - 2 * sign) * (n - s + 1)
                    b, total = paired(q, o, u)
                    if s > 1:
                        ring_copy(q, sign, u, s - 1, b).wait_recv()
                        total = total + ring_in[q, sign, u, s - 2].astype(F32)
                    term[q, b, u] = total.astype(BF16)
                    start(ring_copy(q, sign, u, s, b))

    def column(h, xo, yo, lo=0, n=8):
        yy = mod(y + yo, 8)
        return weight.at[h, pl.ds(lo, n), lax.div(yy, 4), mod(x + xo, NX), lax.rem(yy, 4)]

    columns = (0, -1, 1, -2, 2, -3, 3, 4)

    def send_x(j):
        col = column(c, 0, columns[j])
        for sign in range(2):
            start(copy_to(col, col, gx_s.at[sign, j], gx_r.at[sign, j], along_x(1 - 2 * sign)))

    def gather_y(s):
        for sign in range(2):
            lo, n = (0, 8) if s < 4 else (4 * sign, 4)
            col = column(c, 0, -(1 - 2 * sign) * (s - 1), lo, n)
            start(copy_to(col, col, gy_s.at[sign, s - 1], gy_r.at[sign, s - 1], along_y(1 - 2 * sign)))

    def gathered_y(s):
        for sign in range(2):
            lo, n = (0, 8) if s < 4 else (4 * sign, 4)
            col = column(c, 0, -(1 - 2 * sign) * s, lo, n)
            copy_to(col, col, gy_s.at[sign, s - 1], gy_r.at[sign, s - 1], along_y(1 - 2 * sign)).wait_recv()

    ring_step(1)
    for k in range(1, NZ):
        spot = weight.at[c, mod(z - k, NZ), yh, x, yl]
        copy_to(spot, spot, gz_s.at[k - 1], gz_r.at[k - 1], along_z(k)).wait_recv()
    gather_y(1)
    send_x(0)
    ring_step(2)
    gathered_y(1)
    gather_y(2)
    send_x(1)
    send_x(2)
    ring_step(3)
    gathered_y(2)
    gather_y(3)
    send_x(3)
    send_x(4)
    ring_step(4)
    gathered_y(3)
    gather_y(4)
    send_x(5)
    send_x(6)

    for q in range(2):
        for u in range(2):
            b, total = paired(q, 0, u)
            for sign in range(2):
                n = length(sign, u)
                ring_copy(q, sign, u, n, b).wait_recv()
                total = total + ring_in[q, sign, u, n - 1].astype(F32)
            for j in range(4):
                if q == 0:
                    block[q, u * 4 + j] = total.reshape(4, 4, 16, 128)[:, j]
                else:
                    block[q, u * 4 + j] = total[j].reshape(4, 16, 128)
    def block_copy(q, k):
        return copy_to(
            block.at[q, mod(across_place[q] + k, 8)], block_in.at[q, k - 1],
            block_s.at[q, k - 1], block_r.at[q, k - 1], across[q](k),
        )

    for k in (4, 3, 5, 2, 6, 1, 7):
        for q in range(2):
            start(block_copy(q, k))

    gathered_y(4)
    send_x(7)

    def to_sibling(i, xo):
        part = weight.at[c, :, :, mod(x + xo, NX)]
        start(copy_to(part, part, gc_s.at[i], gc_r.at[i], sibling))

    to_sibling(0, 0)
    for j in range(8):
        for sign in range(2):
            col = column(c, -(1 - 2 * sign), columns[j])
            copy_to(col, col, gx_s.at[sign, j], gx_r.at[sign, j], along_x(1 - 2 * sign)).wait_recv()
            half = column(c, -(1 - 2 * sign), columns[j], 4 * sign, 4)
            start(copy_to(half, half, gf_s.at[sign, j], gf_r.at[sign, j], along_x(1 - 2 * sign)))
    to_sibling(1, -1)
    to_sibling(2, 1)

    for q in range(2):
        total = block[q, across_place[q]]
        for k in range(1, 8):
            block_copy(q, k).wait_recv()
            total = total + block_in[q, k - 1]
        slab[:, q] = total

    def slab_copy(k):
        return copy_to(slab.at[mod(x + k, NX)], slab_in.at[k - 1], slab_s.at[k - 1], slab_r.at[k - 1], along_x(k))

    for k in range(1, NX):
        start(slab_copy(k))

    for j in range(8):
        for sign in range(2):
            half = column(c, 2, columns[j], 4 * sign, 4)
            copy_to(half, half, gf_s.at[sign, j], gf_r.at[sign, j], along_x(1 - 2 * sign)).wait_recv()
    to_sibling(3, 2)

    total = slab[x]
    for k in range(1, NX):
        slab_copy(k).wait_recv()
        total = total + slab_in[k - 1]
    mine[0] = total[:, :8]
    mine[1] = total[:, 8:]
    start(copy_to(mine.at[sib], mine_in, mine_s, mine_r, sibling))

    sq = total * total
    sq = sq[0, :8] + sq[0, 8:] + sq[1, :8] + sq[1, 8:]

    def multiply(lo, hi):
        def one(zb, carry):
            at = pl.ds(pl.multiple_of(zb * 512, 512), 512)
            rows = x_ref[:, at]
            w0 = weight[0, zb].reshape(512, 256)
            w1 = weight[1, zb].reshape(512, 256)
            k0 = jnp.dot(rows, w0, preferred_element_type=F32)
            k1 = jnp.dot(rows, w1, preferred_element_type=F32)

            @pl.when(zb == 0)
            def _():
                keys_sum[:, :256] = k0
                keys_sum[:, 256:] = k1

            @pl.when(zb > 0)
            def _():
                keys_sum[:, :256] += k0
                keys_sum[:, 256:] += k1

            nt = (((1,), (1,)), ((), ()))
            g = lax.dot_general(c_ref[:, :256], w0, nt, preferred_element_type=F32)
            g += lax.dot_general(c_ref[:, 256:], w1, nt, preferred_element_type=F32)
            grad_ref[:, at] = g.astype(BF16)
            return carry

        lax.fori_loop(lo, hi, one, 0)

    groups = (
        [dev(mod(x + k, NX), y, z, mod(c + j, 2)) for k in range(NX) for j in range(2) if k or j],
        [along_y(k) for k in range(1, NY)],
        [along_z(k) for k in range(1, NZ)],
    )

    def square_copy(i, k):
        return copy_to(squares.at[i], squares_in.at[i, k], sq_s.at[i, k], sq_r.at[i, k], groups[i][k])

    parts = ((0, 3), (3, 6), (6, 8))
    for i in range(3):
        squares[i] = sq
        for k in range(7):
            start(square_copy(i, k))
        if i == 0:
            for n, xo in enumerate((0, -1, 1, 2)):
                part = weight.at[sib, :, :, mod(x + xo, NX)]
                copy_to(part, part, gc_s.at[n], gc_r.at[n], sibling).wait_recv()
        multiply(*parts[i])
        if i == 2:
            keys_ref[...] = keys_sum[...].astype(BF16)
        for k in range(7):
            square_copy(i, k).wait_recv()
            sq = sq + squares_in[i, k]

    scale = lax.rsqrt(jnp.full((8, 128), jnp.sum(sq) / 2097152.0 + 1e-06, F32))
    copy_to(mine.at[sib], mine_in, mine_s, mine_r, sibling).wait_recv()
    got = mine[c]
    came = mine_in[...]
    for q in range(2):
        update_ref[:, q * 128 : q * 128 + 128] = jnp.where(c == 0, got[q], came[q]) * scale
        update_ref[:, 256 + q * 128 : 384 + q * 128] = jnp.where(c == 0, came[q], got[q]) * scale
    for copy in sent:
        copy.wait_send()


def body(normed_input, key_weight, key_cotangent):
    vmem = pl.BlockSpec(memory_space=pltpu.VMEM)
    dma = pltpu.SemaphoreType.DMA
    return pl.pallas_call(
        kernel,
        out_shape=(
            jax.ShapeDtypeStruct((256, 512), BF16),
            jax.ShapeDtypeStruct((256, 4096), BF16),
            jax.ShapeDtypeStruct((8, 512), F32),
        ),
        in_specs=[vmem] * 3,
        out_specs=(vmem,) * 3,
        scratch_shapes=[
            pltpu.VMEM((2, NZ, 2, NX, 4, 16, 256), BF16),
            pltpu.VMEM((2, 8, 256), F32),
            pltpu.VMEM((8, 256), F32),
            pltpu.VMEM((2, 8, 2, 4, 64, 128), BF16),
            pltpu.VMEM((2, 8, 2, 4, 64, 128), BF16),
            pltpu.VMEM((2, 8, 2, 4, 64, 128), BF16),
            pltpu.VMEM((2, 2, 2, 4, 4, 64, 128), BF16),
            pltpu.VMEM((2, 8, 4, 16, 128), F32),
            pltpu.VMEM((2, 7, 4, 16, 128), F32),
            pltpu.VMEM((4, 2, 16, 128), F32),
            pltpu.VMEM((3, 2, 16, 128), F32),
            pltpu.VMEM((2, 2, 8, 128), F32),
            pltpu.VMEM((2, 8, 128), F32),
            pltpu.VMEM((3, 8, 128), F32),
            pltpu.VMEM((3, 7, 8, 128), F32),
            pltpu.VMEM((256, 512), F32),
            dma, dma, dma((2, 8)), dma((2, 8)), dma((7,)), dma((7,)), dma((2, 4)), dma((2, 4)),
            dma((2, 8)), dma((2, 8)), dma((2, 8)), dma((2, 8)), dma((4,)), dma((4,)),
            dma((2, 2, 2, 4)), dma((2, 2, 2, 4)), dma((2, 7)), dma((2, 7)), dma((3,)), dma((3,)),
            dma, dma, dma((3, 7)), dma((3, 7)),
        ],
        compiler_params=pltpu.CompilerParams(
            collective_id=0, has_side_effects=True, vmem_limit_bytes=50 * 2**20
        ),
        cost_estimate=pl.CostEstimate(flops=3_221_225_472, bytes_accessed=5_000_000, transcendentals=0),
    )(normed_input, key_weight, key_cotangent)


def solution(mesh):
    placed = P(("node", "local"), None)
    return jax.shard_map(
        body, mesh=mesh, in_specs=(placed,) * 3, out_specs=(placed,) * 3, check_vma=False
    )
```

```python
import jax
import jax.numpy as jnp
from jax import lax
from jax.experimental import pallas as pl
from jax.experimental.pallas import tpu as pltpu
from jax.sharding import PartitionSpec as P

MESH = pl.DeviceIdType.MESH
NX, NY, NZ = 4, 8, 8
F32, BF16 = jnp.float32, jnp.bfloat16
ORDER = (4, 3, 5, 2, 6, 1, 7, 0)


def mod(a, n):
    return lax.rem(a + n, n)


def dev(x, y, z, c):
    return ((z * 2 + lax.div(y, 4)) * 4 + x, lax.rem(y, 4) * 2 + c)


def copy_to(src, dst, send_sem, recv_sem, device):
    return pltpu.make_async_remote_copy(
        src_ref=src,
        dst_ref=dst,
        send_sem=send_sem,
        recv_sem=recv_sem,
        device_id=device,
        device_id_type=MESH,
    )


def kernel(
    x_hbm, w_hbm, c_hbm, keys_ref, grad_ref, update_ref,
    x_ref, w_ref, c_ref, in_s, weight, shard, shard_in, away, pair_in, term, ring_in, block, block_in,
    slab, slab_in, mine, mine_in, squares, squares_in, keys_sum,
    shard_s, shard_r, pair_s, pair_r, gz_s, gz_r, gy_s, gy_r, gx_s, gx_r, gf_s, gf_r, gc_s, gc_r,
    ring_s, ring_r, block_s, block_r, slab_s, slab_r, mine_s, mine_r, sq_s, sq_r,
):
    node, local = lax.axis_index("node"), lax.axis_index("local")
    x = lax.rem(node, 4)
    y = lax.rem(lax.div(node, 4), 2) * 4 + lax.div(local, 2)
    z = lax.div(node, 8)
    c = lax.rem(local, 2)
    sib = 1 - c
    sibling = dev(x, y, z, sib)
    along_x = lambda k: dev(mod(x + k, NX), y, z, c)
    along_y = lambda k: dev(x, mod(y + k, NY), z, c)
    along_z = lambda k: dev(x, y, mod(z + k, NZ), c)
    place = (z, y)
    along = (along_z, along_y)
    across = (along_y, along_z)
    across_place = (y, z)
    sent = []

    def start(copy):
        copy.start()
        sent.append(copy)

    barrier = pltpu.get_barrier_semaphore()
    greeted = [along_z(k) for k in range(1, NZ)] + [along_y(k) for k in range(1, NY)]
    greeted += [dev(mod(x + k, NX), y, z, c) for k in range(1, NX)]
    greeted += [dev(mod(x + k, NX), y, z, sib) for k in range(NX)]
    for device in greeted:
        pl.semaphore_signal(barrier, inc=1, device_id=device, device_id_type=MESH)

    loads = [
        pltpu.make_async_copy(c_hbm, c_ref, in_s.at[0]),
        pltpu.make_async_copy(w_hbm, w_ref, in_s.at[1]),
    ]
    for i in range(4):
        at = pl.ds(i * 1024, 1024)
        loads.append(pltpu.make_async_copy(x_hbm.at[:, at], x_ref.at[:, at], in_s.at[2 + i]))
    for load in loads:
        load.start()

    def terms_of(half, ref, lo, hi):
        cot = c_ref[:, pl.ds(pl.multiple_of(half * 256, 256), 256)]

        def one(zb, carry):
            rows = x_ref[:, pl.ds(pl.multiple_of(zb * 512, 512), 512)]
            t = lax.dot_general(
                rows, cot, (((0,), (0,)), ((), ())), preferred_element_type=F32
            ).astype(BF16)
            ref[0, zb] = t[:, :128].reshape(4, 2, 64, 128)
            tb = t[:, 128:].reshape(2, 4, 4, 16, 128)
            for yh in range(2):
                for yl in range(4):
                    ref[1, yh * 4 + yl, lax.div(zb, 2), lax.rem(zb, 2)] = tb[yh, :, yl].reshape(64, 128)
            return carry

        lax.fori_loop(lo, hi, one, 0)

    loads[0].wait()
    loads[1].wait()
    w = w_ref[...].astype(F32)
    shard[0] = w[:, :256]
    shard[1] = w[:, 256:]
    for i in range(4):
        loads[2 + i].wait()
        terms_of(sib, away, 2 * i, 2 * i + 2)
    pl.semaphore_wait(barrier, len(greeted))

    start(copy_to(shard.at[sib], shard_in, shard_s, shard_r, sibling))
    pairs = {}
    for o in ORDER:
        for q in range(2):
            b = mod(place[q] + o, 8)
            pairs[q, o] = copy_to(away.at[q, b], pair_in.at[q, b], pair_s.at[q, o], pair_r.at[q, o], sibling)
            start(pairs[q, o])

    yh, yl = lax.div(y, 4), lax.rem(y, 4)
    copy_to(shard.at[sib], shard_in, shard_s, shard_r, sibling).wait_recv()
    own, other = shard[c], shard_in[...]
    first = jnp.where(c == 0, own, other)
    second = jnp.where(c == 0, other, own)
    weight[c, z, yh, x, yl] = jnp.concatenate([first, second], axis=0).astype(BF16)
    for k in range(1, NZ):
        spot = weight.at[c, z, yh, x, yl]
        start(copy_to(spot, spot, gz_s.at[k - 1], gz_r.at[k - 1], along_z(k)))

    terms_of(c, term, 0, 8)

    def part_of(sign, v):
        return v if sign == 0 else lax.rem(v + 2, 4)

    def ring_copy(q, sign, v, s, b):
        return copy_to(
            term.at[q, b, part_of(sign, v)],
            ring_in.at[q, sign, v, s - 1],
            ring_s.at[q, sign, v, s - 1],
            ring_r.at[q, sign, v, s - 1],
            along[q](1 - 2 * sign),
        )

    def pair_wait(*offsets):
        for o in offsets:
            for q in range(2):
                pairs[q, o].wait_recv()

    def ring_step(s, far):
        n = 4 if far else 3

        def one(i, carry):
            v = i if far else i + 2
            for q in range(2):
                for sign in range(2):
                    b = mod(place[q] + (1 - 2 * sign) * (n - s + 1), 8)
                    u = part_of(sign, v)
                    total = term[q, b, u].astype(F32) + pair_in[q, b, u].astype(F32)
                    if s > 1:
                        ring_copy(q, sign, v, s - 1, b).wait_recv()
                        total = total + ring_in[q, sign, v, s - 2].astype(F32)
                    term[q, b, u] = total.astype(BF16)
                    ring_copy(q, sign, v, s, b).start()
            return carry

        lax.fori_loop(0, 2, one, 0)

    def ring_sent():
        for s in range(1, 5):
            def one(v, carry):
                for q in range(2):
                    for sign in range(2):
                        ring_copy(q, sign, v, s, 0).wait_send()
                return carry

            lax.fori_loop(0, 4 if s < 4 else 2, one, 0)

    def column(h, xo, yo, lo=0, n=8):
        yy = mod(y + yo, 8)
        return weight.at[h, pl.ds(lo, n), lax.div(yy, 4), mod(x + xo, NX), lax.rem(yy, 4)]

    columns = (0, -1, 1, -2, 2, -3, 3, 4)

    def send_x(j):
        col = column(c, 0, columns[j])
        for sign in range(2):
            start(copy_to(col, col, gx_s.at[sign, j], gx_r.at[sign, j], along_x(1 - 2 * sign)))

    def gather_y(s):
        for sign in range(2):
            lo, n = (0, 8) if s < 4 else (4 * sign, 4)
            col = column(c, 0, -(1 - 2 * sign) * (s - 1), lo, n)
            start(copy_to(col, col, gy_s.at[sign, s - 1], gy_r.at[sign, s - 1], along_y(1 - 2 * sign)))

    def gathered_y(s):
        for sign in range(2):
            lo, n = (0, 8) if s < 4 else (4 * sign, 4)
            col = column(c, 0, -(1 - 2 * sign) * s, lo, n)
            copy_to(col, col, gy_s.at[sign, s - 1], gy_r.at[sign, s - 1], along_y(1 - 2 * sign)).wait_recv()

    def to_sibling(i, xo):
        part = weight.at[c, :, :, mod(x + xo, NX)]
        start(copy_to(part, part, gc_s.at[i], gc_r.at[i], sibling))

    def forward_x(j):
        for sign in range(2):
            col = column(c, -(1 - 2 * sign), columns[j])
            copy_to(col, col, gx_s.at[sign, j], gx_r.at[sign, j], along_x(1 - 2 * sign)).wait_recv()
            half = column(c, -(1 - 2 * sign), columns[j], 4 * sign, 4)
            start(copy_to(half, half, gf_s.at[sign, j], gf_r.at[sign, j], along_x(1 - 2 * sign)))

    pair_wait(4)
    ring_step(1, True)
    pair_wait(3, 5)
    ring_step(1, False)
    for k in range(1, NZ):
        spot = weight.at[c, mod(z - k, NZ), yh, x, yl]
        copy_to(spot, spot, gz_s.at[k - 1], gz_r.at[k - 1], along_z(k)).wait_recv()
    gather_y(1)
    send_x(0)
    ring_step(2, True)
    pair_wait(2, 6)
    ring_step(2, False)
    gathered_y(1)
    gather_y(2)
    send_x(1)
    send_x(2)
    ring_step(3, True)
    pair_wait(1, 7)
    ring_step(3, False)
    gathered_y(2)
    gather_y(3)
    send_x(3)
    send_x(4)
    forward_x(0)
    ring_step(4, True)
    gathered_y(3)
    gather_y(4)
    send_x(5)
    send_x(6)
    forward_x(1)
    forward_x(2)

    pair_wait(0)
    for v in range(4):
        for q in range(2):
            total = term[q, place[q], v].astype(F32) + pair_in[q, place[q], v].astype(F32)
            for sign in range(2):
                w_ = v if sign == 0 else (v + 2) % 4
                n = 4 if w_ < 2 else 3
                ring_copy(q, sign, w_, n, 0).wait_recv()
                total = total + ring_in[q, sign, w_, n - 1].astype(F32)
            if q == 0:
                for yl in range(4):
                    block[0, (v // 2) * 4 + yl, (v % 2) * 2 : (v % 2) * 2 + 2] = total.reshape(2, 4, 16, 128)[:, yl]
            else:
                block[1, 2 * v : 2 * v + 2] = total.reshape(2, 4, 16, 128)

    def block_copy(q, k):
        return copy_to(
            block.at[q, mod(across_place[q] + k, 8)], block_in.at[q, k - 1],
            block_s.at[q, k - 1], block_r.at[q, k - 1], across[q](k),
        )

    for k in (4, 3, 5, 2, 6, 1, 7):
        for q in range(2):
            start(block_copy(q, k))

    gathered_y(4)
    send_x(7)
    to_sibling(0, 0)
    forward_x(3)
    forward_x(4)

    for q in range(2):
        total = block[q, across_place[q]]
        for k in range(1, 8):
            block_copy(q, k).wait_recv()
            total = total + block_in[q, k - 1]
        slab[:, q] = total

    def slab_copy(k):
        return copy_to(slab.at[mod(x + k, NX)], slab_in.at[k - 1], slab_s.at[k - 1], slab_r.at[k - 1], along_x(k))

    for k in range(1, NX):
        start(slab_copy(k))
    for j in range(5, 8):
        forward_x(j)
    to_sibling(1, -1)
    to_sibling(2, 1)

    total = slab[x]
    for k in range(1, NX):
        slab_copy(k).wait_recv()
        total = total + slab_in[k - 1]
    mine[0] = total[:, :8]
    mine[1] = total[:, 8:]
    start(copy_to(mine.at[sib], mine_in, mine_s, mine_r, sibling))

    sq = total * total
    sq = sq[0, :8] + sq[0, 8:] + sq[1, :8] + sq[1, 8:]

    def multiply(lo, hi):
        def one(zb, carry):
            at = pl.ds(pl.multiple_of(zb * 512, 512), 512)
            rows = x_ref[:, at]
            w0 = weight[0, zb].reshape(512, 256)
            w1 = weight[1, zb].reshape(512, 256)
            k0 = jnp.dot(rows, w0, preferred_element_type=F32)
            k1 = jnp.dot(rows, w1, preferred_element_type=F32)

            @pl.when(zb == 0)
            def _():
                keys_sum[:, :256] = k0
                keys_sum[:, 256:] = k1

            @pl.when(zb > 0)
            def _():
                keys_sum[:, :256] += k0
                keys_sum[:, 256:] += k1

            nt = (((1,), (1,)), ((), ()))
            g = lax.dot_general(c_ref[:, :256], w0, nt, preferred_element_type=F32)
            g += lax.dot_general(c_ref[:, 256:], w1, nt, preferred_element_type=F32)
            grad_ref[:, at] = g.astype(BF16)
            return carry

        lax.fori_loop(lo, hi, one, 0)

    groups = (
        [dev(mod(x + k, NX), y, z, mod(c + j, 2)) for k in range(NX) for j in range(2) if k or j],
        [along_y(k) for k in range(1, NY)],
        [along_z(k) for k in range(1, NZ)],
    )

    def square_copy(i, k):
        return copy_to(squares.at[i], squares_in.at[i, k], sq_s.at[i, k], sq_r.at[i, k], groups[i][k])

    def square_send(i):
        squares[i] = sq
        for k in range(7):
            start(square_copy(i, k))

    def square_sum(i, sq):
        for k in range(7):
            square_copy(i, k).wait_recv()
            sq = sq + squares_in[i, k]
        return sq

    square_send(0)
    for j in range(8):
        for sign in range(2):
            half = column(c, 2, columns[j], 4 * sign, 4)
            copy_to(half, half, gf_s.at[sign, j], gf_r.at[sign, j], along_x(1 - 2 * sign)).wait_recv()
    to_sibling(3, 2)
    sq = square_sum(0, sq)
    square_send(1)
    for n, xo in enumerate((0, -1, 1, 2)):
        part = weight.at[sib, :, :, mod(x + xo, NX)]
        copy_to(part, part, gc_s.at[n], gc_r.at[n], sibling).wait_recv()
    multiply(0, 5)
    sq = square_sum(1, sq)
    square_send(2)
    multiply(5, 8)
    keys_ref[...] = keys_sum[...].astype(BF16)
    ring_sent()
    for copy in sent[:-7]:
        copy.wait_send()
    sq = square_sum(2, sq)

    scale = lax.rsqrt(jnp.full((8, 128), jnp.sum(sq) / 2097152.0 + 1e-06, F32))
    copy_to(mine.at[sib], mine_in, mine_s, mine_r, sibling).wait_recv()
    got = mine[c]
    came = mine_in[...]
    for q in range(2):
        update_ref[:, q * 128 : q * 128 + 128] = jnp.where(c == 0, got[q], came[q]) * scale
        update_ref[:, 256 + q * 128 : 384 + q * 128] = jnp.where(c == 0, came[q], got[q]) * scale
    for copy in sent[-7:]:
        copy.wait_send()


def body(normed_input, key_weight, key_cotangent):
    vmem = pl.BlockSpec(memory_space=pltpu.VMEM)
    dma = pltpu.SemaphoreType.DMA
    return pl.pallas_call(
        kernel,
        out_shape=(
            jax.ShapeDtypeStruct((256, 512), BF16),
            jax.ShapeDtypeStruct((256, 4096), BF16),
            jax.ShapeDtypeStruct((8, 512), F32),
        ),
        in_specs=[pl.BlockSpec(memory_space=pltpu.HBM)] * 3,
        out_specs=(vmem,) * 3,
        scratch_shapes=[
            pltpu.VMEM((256, 4096), BF16),
            pltpu.VMEM((8, 512), BF16),
            pltpu.VMEM((256, 512), BF16),
            dma((6,)),
            pltpu.VMEM((2, NZ, 2, NX, 4, 16, 256), BF16),
            pltpu.VMEM((2, 8, 256), F32),
            pltpu.VMEM((8, 256), F32),
            pltpu.VMEM((2, 8, 4, 2, 64, 128), BF16),
            pltpu.VMEM((2, 8, 4, 2, 64, 128), BF16),
            pltpu.VMEM((2, 8, 4, 2, 64, 128), BF16),
            pltpu.VMEM((2, 2, 4, 4, 2, 64, 128), BF16),
            pltpu.VMEM((2, 8, 4, 16, 128), F32),
            pltpu.VMEM((2, 7, 4, 16, 128), F32),
            pltpu.VMEM((4, 2, 16, 128), F32),
            pltpu.VMEM((3, 2, 16, 128), F32),
            pltpu.VMEM((2, 2, 8, 128), F32),
            pltpu.VMEM((2, 8, 128), F32),
            pltpu.VMEM((3, 8, 128), F32),
            pltpu.VMEM((3, 7, 8, 128), F32),
            pltpu.VMEM((256, 512), F32),
            dma, dma, dma((2, 8)), dma((2, 8)), dma((7,)), dma((7,)), dma((2, 4)), dma((2, 4)),
            dma((2, 8)), dma((2, 8)), dma((2, 8)), dma((2, 8)), dma((4,)), dma((4,)),
            dma((2, 2, 4, 4)), dma((2, 2, 4, 4)), dma((2, 7)), dma((2, 7)), dma((3,)), dma((3,)),
            dma, dma, dma((3, 7)), dma((3, 7)),
        ],
        compiler_params=pltpu.CompilerParams(
            collective_id=0, has_side_effects=True, vmem_limit_bytes=50 * 2**20
        ),
        cost_estimate=pl.CostEstimate(flops=3_221_225_472, bytes_accessed=5_000_000, transcendentals=0),
    )(normed_input, key_weight, key_cotangent)


def solution(mesh):
    placed = P(("node", "local"), None)
    return jax.shard_map(
        body, mesh=mesh, in_specs=(placed,) * 3, out_specs=(placed,) * 3, check_vma=False
    )
```

```python
import jax
import jax.numpy as jnp
from jax import lax
from jax.experimental import pallas as pl
from jax.experimental.pallas import tpu as pltpu
from jax.sharding import PartitionSpec as P

MESH = pl.DeviceIdType.MESH
NX, NY, NZ = 4, 8, 8
F32, BF16 = jnp.float32, jnp.bfloat16
ORDER = (4, 3, 5, 2, 6, 1, 7, 0)


def mod(a, n):
    return lax.rem(a + n, n)


def dev(x, y, z, c):
    return ((z * 2 + lax.div(y, 4)) * 4 + x, lax.rem(y, 4) * 2 + c)


def copy_to(src, dst, send_sem, recv_sem, device):
    return pltpu.make_async_remote_copy(
        src_ref=src,
        dst_ref=dst,
        send_sem=send_sem,
        recv_sem=recv_sem,
        device_id=device,
        device_id_type=MESH,
    )


def kernel(
    x_hbm, w_hbm, c_hbm, keys_ref, grad_ref, update_ref,
    x_ref, w_ref, c_ref, in_s, weight, shard, shard_in, away, pair_in, term, ring_in, block, block_in,
    slab, slab_in, mine, mine_in, squares, squares_in, keys_sum,
    shard_s, shard_r, pair_s, pair_r, gz_s, gz_r, gy_s, gy_r, gx_s, gx_r, gf_s, gf_r, gc_s, gc_r,
    ring_s, ring_r, block_s, block_r, slab_s, slab_r, mine_s, mine_r, sq_s, sq_r,
):
    node, local = lax.axis_index("node"), lax.axis_index("local")
    x = lax.rem(node, 4)
    y = lax.rem(lax.div(node, 4), 2) * 4 + lax.div(local, 2)
    z = lax.div(node, 8)
    c = lax.rem(local, 2)
    sib = 1 - c
    sibling = dev(x, y, z, sib)
    along_x = lambda k: dev(mod(x + k, NX), y, z, c)
    along_y = lambda k: dev(x, mod(y + k, NY), z, c)
    along_z = lambda k: dev(x, y, mod(z + k, NZ), c)
    place = (z, y)
    along = (along_z, along_y)
    across = (along_y, along_z)
    across_place = (y, z)
    sent = []

    def start(copy):
        copy.start()
        sent.append(copy)

    barrier = pltpu.get_barrier_semaphore()
    greeted = [along_z(k) for k in range(1, NZ)] + [along_y(k) for k in range(1, NY)]
    greeted += [dev(mod(x + k, NX), y, z, c) for k in range(1, NX)]
    greeted += [dev(mod(x + k, NX), y, z, sib) for k in range(NX)]
    for device in greeted:
        pl.semaphore_signal(barrier, inc=1, device_id=device, device_id_type=MESH)

    loads = [
        pltpu.make_async_copy(c_hbm, c_ref, in_s.at[0]),
        pltpu.make_async_copy(w_hbm, w_ref, in_s.at[1]),
    ]
    for i in range(4):
        at = pl.ds(i * 1024, 1024)
        loads.append(pltpu.make_async_copy(x_hbm.at[:, at], x_ref.at[:, at], in_s.at[2 + i]))
    for load in loads:
        load.start()

    def terms_of(half, ref, lo, hi):
        cot = c_ref[:, pl.ds(pl.multiple_of(half * 256, 256), 256)]

        def one(zb, carry):
            rows = x_ref[:, pl.ds(pl.multiple_of(zb * 512, 512), 512)]
            t = lax.dot_general(
                rows, cot, (((0,), (0,)), ((), ())), preferred_element_type=F32
            ).astype(BF16)
            ref[0, zb] = t[:, :128].reshape(4, 2, 64, 128)
            tb = t[:, 128:].reshape(2, 4, 4, 16, 128)
            for yh in range(2):
                for yl in range(4):
                    ref[1, yh * 4 + yl, lax.div(zb, 2), lax.rem(zb, 2)] = tb[yh, :, yl].reshape(64, 128)
            return carry

        lax.fori_loop(lo, hi, one, 0)

    loads[0].wait()
    loads[1].wait()
    w = w_ref[...].astype(F32)
    shard[0] = w[:, :256]
    shard[1] = w[:, 256:]
    for i in range(4):
        loads[2 + i].wait()
        terms_of(sib, away, 2 * i, 2 * i + 2)
    pl.semaphore_wait(barrier, len(greeted))

    start(copy_to(shard.at[sib], shard_in, shard_s, shard_r, sibling))
    pairs = {}
    for o in ORDER:
        for q in range(2):
            b = mod(place[q] + o, 8)
            pairs[q, o] = copy_to(away.at[q, b], pair_in.at[q, b], pair_s.at[q, o], pair_r.at[q, o], sibling)
            start(pairs[q, o])

    yh, yl = lax.div(y, 4), lax.rem(y, 4)
    terms_of(c, term, 0, 4)
    copy_to(shard.at[sib], shard_in, shard_s, shard_r, sibling).wait_recv()
    own, other = shard[c], shard_in[...]
    first = jnp.where(c == 0, own, other)
    second = jnp.where(c == 0, other, own)
    weight[c, z, yh, x, yl] = jnp.concatenate([first, second], axis=0).astype(BF16)
    for k in range(1, NZ):
        spot = weight.at[c, z, yh, x, yl]
        start(copy_to(spot, spot, gz_s.at[k - 1], gz_r.at[k - 1], along_z(k)))

    terms_of(c, term, 4, 8)

    def part_of(sign, v):
        return v if sign == 0 else lax.rem(v + 2, 4)

    def ring_copy(q, sign, v, s, b):
        return copy_to(
            term.at[q, b, part_of(sign, v)],
            ring_in.at[q, sign, v, s - 1],
            ring_s.at[q, sign, v, s - 1],
            ring_r.at[q, sign, v, s - 1],
            along[q](1 - 2 * sign),
        )

    def pair_wait(*offsets):
        for o in offsets:
            for q in range(2):
                pairs[q, o].wait_recv()

    def ring_step(s, far):
        n = 4 if far else 3

        def one(i, carry):
            v = i if far else i + 2
            for q in range(2):
                for sign in range(2):
                    b = mod(place[q] + (1 - 2 * sign) * (n - s + 1), 8)
                    u = part_of(sign, v)
                    total = term[q, b, u].astype(F32) + pair_in[q, b, u].astype(F32)
                    if s > 1:
                        ring_copy(q, sign, v, s - 1, b).wait_recv()
                        total = total + ring_in[q, sign, v, s - 2].astype(F32)
                    term[q, b, u] = total.astype(BF16)
                    ring_copy(q, sign, v, s, b).start()
            return carry

        lax.fori_loop(0, 2, one, 0)

    def ring_sent():
        for s in range(1, 5):
            def one(v, carry):
                for q in range(2):
                    for sign in range(2):
                        ring_copy(q, sign, v, s, 0).wait_send()
                return carry

            lax.fori_loop(0, 4 if s < 4 else 2, one, 0)

    def column(h, xo, yo, lo=0, n=8):
        yy = mod(y + yo, 8)
        return weight.at[h, pl.ds(lo, n), lax.div(yy, 4), mod(x + xo, NX), lax.rem(yy, 4)]

    columns = (0, -1, 1, -2, 2, -3, 3, 4)

    def send_x(j):
        col = column(c, 0, columns[j])
        for sign in range(2):
            start(copy_to(col, col, gx_s.at[sign, j], gx_r.at[sign, j], along_x(1 - 2 * sign)))

    def gather_y(s):
        for sign in range(2):
            lo, n = (0, 8) if s < 4 else (4 * sign, 4)
            col = column(c, 0, -(1 - 2 * sign) * (s - 1), lo, n)
            start(copy_to(col, col, gy_s.at[sign, s - 1], gy_r.at[sign, s - 1], along_y(1 - 2 * sign)))

    def gathered_y(s):
        for sign in range(2):
            lo, n = (0, 8) if s < 4 else (4 * sign, 4)
            col = column(c, 0, -(1 - 2 * sign) * s, lo, n)
            copy_to(col, col, gy_s.at[sign, s - 1], gy_r.at[sign, s - 1], along_y(1 - 2 * sign)).wait_recv()

    def to_sibling(i, xo):
        part = weight.at[c, :, :, mod(x + xo, NX)]
        start(copy_to(part, part, gc_s.at[i], gc_r.at[i], sibling))

    def forward_x(j):
        for sign in range(2):
            col = column(c, -(1 - 2 * sign), columns[j])
            copy_to(col, col, gx_s.at[sign, j], gx_r.at[sign, j], along_x(1 - 2 * sign)).wait_recv()
            half = column(c, -(1 - 2 * sign), columns[j], 4 * sign, 4)
            start(copy_to(half, half, gf_s.at[sign, j], gf_r.at[sign, j], along_x(1 - 2 * sign)))

    pair_wait(4)
    ring_step(1, True)
    pair_wait(3, 5)
    ring_step(1, False)
    for k in range(1, NZ):
        spot = weight.at[c, mod(z - k, NZ), yh, x, yl]
        copy_to(spot, spot, gz_s.at[k - 1], gz_r.at[k - 1], along_z(k)).wait_recv()
    gather_y(1)
    send_x(0)
    ring_step(2, True)
    pair_wait(2, 6)
    ring_step(2, False)
    gathered_y(1)
    gather_y(2)
    send_x(1)
    send_x(2)
    ring_step(3, True)
    pair_wait(1, 7)
    ring_step(3, False)
    gathered_y(2)
    gather_y(3)
    send_x(3)
    send_x(4)
    forward_x(0)
    ring_step(4, True)
    gathered_y(3)
    gather_y(4)
    send_x(5)
    send_x(6)
    forward_x(1)
    forward_x(2)

    pair_wait(0)
    for v in range(4):
        for q in range(2):
            total = term[q, place[q], v].astype(F32) + pair_in[q, place[q], v].astype(F32)
            for sign in range(2):
                w_ = v if sign == 0 else (v + 2) % 4
                n = 4 if w_ < 2 else 3
                ring_copy(q, sign, w_, n, 0).wait_recv()
                total = total + ring_in[q, sign, w_, n - 1].astype(F32)
            if q == 0:
                for yl in range(4):
                    block[0, (v // 2) * 4 + yl, (v % 2) * 2 : (v % 2) * 2 + 2] = total.reshape(2, 4, 16, 128)[:, yl]
            else:
                block[1, 2 * v : 2 * v + 2] = total.reshape(2, 4, 16, 128)

    def block_copy(q, k):
        return copy_to(
            block.at[q, mod(across_place[q] + k, 8)], block_in.at[q, k - 1],
            block_s.at[q, k - 1], block_r.at[q, k - 1], across[q](k),
        )

    for k in (4, 3, 5, 2, 6, 1, 7):
        for q in range(2):
            start(block_copy(q, k))

    gathered_y(4)
    send_x(7)
    to_sibling(0, 0)
    forward_x(3)
    forward_x(4)

    for q in range(2):
        total = block[q, across_place[q]]
        for k in range(1, 8):
            block_copy(q, k).wait_recv()
            total = total + block_in[q, k - 1]
        slab[:, q] = total

    def slab_copy(k):
        return copy_to(slab.at[mod(x + k, NX)], slab_in.at[k - 1], slab_s.at[k - 1], slab_r.at[k - 1], along_x(k))

    for k in range(1, NX):
        start(slab_copy(k))
    for j in range(5, 8):
        forward_x(j)
    to_sibling(1, -1)
    to_sibling(2, 1)

    total = slab[x]
    for k in range(1, NX):
        slab_copy(k).wait_recv()
        total = total + slab_in[k - 1]
    mine[0] = total[:, :8]
    mine[1] = total[:, 8:]
    start(copy_to(mine.at[sib], mine_in, mine_s, mine_r, sibling))

    sq = total * total
    sq = sq[0, :8] + sq[0, 8:] + sq[1, :8] + sq[1, 8:]

    def multiply(lo, hi):
        def one(zb, carry):
            at = pl.ds(pl.multiple_of(zb * 512, 512), 512)
            rows = x_ref[:, at]
            w0 = weight[0, zb].reshape(512, 256)
            w1 = weight[1, zb].reshape(512, 256)
            k0 = jnp.dot(rows, w0, preferred_element_type=F32)
            k1 = jnp.dot(rows, w1, preferred_element_type=F32)

            @pl.when(zb == 0)
            def _():
                keys_sum[:, :256] = k0
                keys_sum[:, 256:] = k1

            @pl.when(zb > 0)
            def _():
                keys_sum[:, :256] += k0
                keys_sum[:, 256:] += k1

            nt = (((1,), (1,)), ((), ()))
            g = lax.dot_general(c_ref[:, :256], w0, nt, preferred_element_type=F32)
            g += lax.dot_general(c_ref[:, 256:], w1, nt, preferred_element_type=F32)
            grad_ref[:, at] = g.astype(BF16)
            return carry

        lax.fori_loop(lo, hi, one, 0)

    groups = (
        [dev(mod(x + k, NX), y, z, mod(c + j, 2)) for k in range(NX) for j in range(2) if k or j],
        [along_y(k) for k in range(1, NY)],
        [along_z(k) for k in range(1, NZ)],
    )

    def square_copy(i, k):
        return copy_to(squares.at[i], squares_in.at[i, k], sq_s.at[i, k], sq_r.at[i, k], groups[i][k])

    def square_send(i):
        squares[i] = sq
        for k in range(7):
            start(square_copy(i, k))

    def square_sum(i, sq):
        for k in range(7):
            square_copy(i, k).wait_recv()
            sq = sq + squares_in[i, k]
        return sq

    square_send(0)
    for j in range(8):
        for sign in range(2):
            half = column(c, 2, columns[j], 4 * sign, 4)
            copy_to(half, half, gf_s.at[sign, j], gf_r.at[sign, j], along_x(1 - 2 * sign)).wait_recv()
        col = column(c, 2, columns[j])
        start(copy_to(col, col, gc_s.at[3 + j], gc_r.at[3 + j], sibling))
    sq = square_sum(0, sq)
    square_send(1)
    for n, xo in enumerate((0, -1, 1)):
        part = weight.at[sib, :, :, mod(x + xo, NX)]
        copy_to(part, part, gc_s.at[n], gc_r.at[n], sibling).wait_recv()
    for j in range(8):
        col = column(sib, 2, columns[j])
        copy_to(col, col, gc_s.at[3 + j], gc_r.at[3 + j], sibling).wait_recv()
    multiply(0, 5)
    sq = square_sum(1, sq)
    square_send(2)
    multiply(5, 8)
    keys_ref[...] = keys_sum[...].astype(BF16)
    ring_sent()
    for copy in sent[:-7]:
        copy.wait_send()
    sq = square_sum(2, sq)

    scale = lax.rsqrt(jnp.full((8, 128), jnp.sum(sq) / 2097152.0 + 1e-06, F32))
    copy_to(mine.at[sib], mine_in, mine_s, mine_r, sibling).wait_recv()
    got = mine[c]
    came = mine_in[...]
    for q in range(2):
        update_ref[:, q * 128 : q * 128 + 128] = jnp.where(c == 0, got[q], came[q]) * scale
        update_ref[:, 256 + q * 128 : 384 + q * 128] = jnp.where(c == 0, came[q], got[q]) * scale
    for copy in sent[-7:]:
        copy.wait_send()


def body(normed_input, key_weight, key_cotangent):
    vmem = pl.BlockSpec(memory_space=pltpu.VMEM)
    dma = pltpu.SemaphoreType.DMA
    return pl.pallas_call(
        kernel,
        out_shape=(
            jax.ShapeDtypeStruct((256, 512), BF16),
            jax.ShapeDtypeStruct((256, 4096), BF16),
            jax.ShapeDtypeStruct((8, 512), F32),
        ),
        in_specs=[pl.BlockSpec(memory_space=pltpu.HBM)] * 3,
        out_specs=(vmem,) * 3,
        scratch_shapes=[
            pltpu.VMEM((256, 4096), BF16),
            pltpu.VMEM((8, 512), BF16),
            pltpu.VMEM((256, 512), BF16),
            dma((6,)),
            pltpu.VMEM((2, NZ, 2, NX, 4, 16, 256), BF16),
            pltpu.VMEM((2, 8, 256), F32),
            pltpu.VMEM((8, 256), F32),
            pltpu.VMEM((2, 8, 4, 2, 64, 128), BF16),
            pltpu.VMEM((2, 8, 4, 2, 64, 128), BF16),
            pltpu.VMEM((2, 8, 4, 2, 64, 128), BF16),
            pltpu.VMEM((2, 2, 4, 4, 2, 64, 128), BF16),
            pltpu.VMEM((2, 8, 4, 16, 128), F32),
            pltpu.VMEM((2, 7, 4, 16, 128), F32),
            pltpu.VMEM((4, 2, 16, 128), F32),
            pltpu.VMEM((3, 2, 16, 128), F32),
            pltpu.VMEM((2, 2, 8, 128), F32),
            pltpu.VMEM((2, 8, 128), F32),
            pltpu.VMEM((3, 8, 128), F32),
            pltpu.VMEM((3, 7, 8, 128), F32),
            pltpu.VMEM((256, 512), F32),
            dma, dma, dma((2, 8)), dma((2, 8)), dma((7,)), dma((7,)), dma((2, 4)), dma((2, 4)),
            dma((2, 8)), dma((2, 8)), dma((2, 8)), dma((2, 8)), dma((11,)), dma((11,)),
            dma((2, 2, 4, 4)), dma((2, 2, 4, 4)), dma((2, 7)), dma((2, 7)), dma((3,)), dma((3,)),
            dma, dma, dma((3, 7)), dma((3, 7)),
        ],
        compiler_params=pltpu.CompilerParams(
            collective_id=0, has_side_effects=True, vmem_limit_bytes=50 * 2**20
        ),
        cost_estimate=pl.CostEstimate(flops=3_221_225_472, bytes_accessed=5_000_000, transcendentals=0),
    )(normed_input, key_weight, key_cotangent)


def solution(mesh):
    placed = P(("node", "local"), None)
    return jax.shard_map(
        body, mesh=mesh, in_specs=(placed,) * 3, out_specs=(placed,) * 3, check_vma=False
    )
```
